256 devices in a mesh: aux: 8 (over z), tile: 32 (over y, x, core).
Axes of the slice: x: 4, y: 4, z: 8, core: 2. Of those that a mesh axis runs over, the one named last changes fastest.
Arguments:
- transformed: bfloat16 [4096, 106496], P('aux', 'tile'), may hold values from -6 to 6
- coupling: bfloat16 [4096, 4096], P('aux'), may hold values from -0.09375 to 0.09375
- block_mask: int32 [32, 32], replicated, may hold values 0 or 1
- density_row: bfloat16 [16384, 128], P('tile'), may hold values from -0.5 to 0.5
- density_col: bfloat16 [16384, 128], P('tile'), may hold values from -0.5 to 0.5
- row_owner: int32 [832, 1], replicated, may hold values from 0 to 31; in each aligned block of 26 rows (0 to 25, 26 to 51, ...) at most 2 rows name the same one
- row_slot: int32 [832, 1], replicated, may hold values from 0 to 3
- col_owner: int32 [832, 1], replicated, may hold values from 0 to 31; in each aligned block of 26 rows (0 to 25, 26 to 51, ...) at most 2 rows name the same one
- col_slot: int32 [832, 1], replicated, may hold values from 0 to 3
Outputs:
- grad_row: float32 [4096, 16384], P('aux', 'tile')
- grad_col: float32 [4096, 16384], P('aux', 'tile')
The draws below stay inside these ranges and needn't reach their ends.
Inputs may be any that keep to these rules, and one draw needn't show every extreme that they name: `row_owner`: among the 26 tiles of one index of tile (aligned blocks of rows), no owner is named more than 2 times, a bound that some block reaches. `col_owner`: as for row_owner.
All inputs are finite; a program needn't handle non-finite values.
Results may differ from the reference program's by a relative error of at most 0.0041.
Values may be sent and summed in bfloat16 or wider, within the bound.
A program may use at most 128 MiB of HBM per device.

```python
import math
import jax
import jax.numpy as jnp
import numpy as np
from jax import lax

NAUX = 4096
TILE = 128
ZBLK = 128
TILES_DEV = 26
BLK_DEV = 4
NT = 832
NBLK = 128
CAP = 2
N_TILE = 32


def touch_ends(drawn, key, least, high):
    longest = drawn.shape.index(max(drawn.shape))
    spots = []
    for shift in (0, 1):
        where = [jax.random.randint(jax.random.fold_in(key, axis), (), 0, length) for axis, length in enumerate(drawn.shape)]
        where[longest] = (where[longest] + shift) % drawn.shape[longest]
        spots.append(tuple(where))
    return drawn.at[spots[0]].set(least).at[spots[1]].set(high)


def steps_of(own_key, shape, split, low, high):
    level = 1.0
    for axis_at, blocks in split:
        draws = jax.random.uniform(jax.random.fold_in(jax.random.fold_in(own_key, 6), axis_at), (blocks,), jnp.float32, low / len(split), high / len(split))
        level = level * jnp.repeat(jnp.exp(draws), shape[axis_at] // blocks).reshape((-1,) + (1,) * (len(shape) - 1 - axis_at))
    return level


def deal_out(rng, own, number, rows, count, top, reach, skew):
    sequence = jax.random.permutation(rng, count)
    crowded, ordinary = load_shares(count, rows * top, reach, skew, True), load_shares(count, rows * top, reach, skew, False)
    places = jnp.arange(count)

    def named(tallies, offset_by):
        used = int((tallies > 0).sum())
        fixed = max(1, used // 4)
        shifted = fixed + (places - fixed + offset_by * (used - fixed)) % max(1, count - fixed)
        return jnp.zeros((count,), jnp.int32).at[sequence[jnp.where(places < fixed, places, shifted)]].set(jnp.asarray(tallies, jnp.int32))

    tallies = jnp.where(number % 4 == 0, named(crowded, number // 4), named(ordinary, number - number // 4 - 1))
    mixed = jax.random.permutation(jax.random.fold_in(own, 3), count)
    source_of, receiver = mixed[0:count // 2 * 2:2], mixed[1:count // 2 * 2:2]
    slack = jnp.minimum(tallies[source_of] - 1, reach - tallies[receiver]) // 2
    slack = jnp.where((source_of == sequence[0]) | (receiver == sequence[0]) | (tallies[receiver] == 0), 0, jnp.maximum(slack, 0))
    shifted = jax.random.randint(jax.random.fold_in(own, 4), (count // 2,), 0, 1 << 20) % (slack + 1)
    tallies = tallies.at[source_of].add(-shifted).at[receiver].add(shifted)
    members = jnp.searchsorted(jnp.cumsum(tallies), jnp.arange(rows * top), side="right").astype(jnp.int32)
    grid = members.reshape(top, rows).T
    grid = grid[jax.random.permutation(jax.random.fold_in(own, 1), rows)]
    offset_by = jax.random.randint(jax.random.fold_in(own, 2), (rows, 1), 0, top)
    return jnp.take_along_axis(grid, (jnp.arange(top)[None, :] + offset_by) % top, axis=1)


def load_shares(count, total, reach, lean, full):
    portions = [(1 << 20) // math.isqrt(grade ** lean) + 1 for grade in range(1, count + 1)]
    largest = reach if full else min(reach, max(-(-total // count), total * portions[0] // sum(portions)))
    least = 1 if total - largest >= count - 1 else 0
    holding, spare = [largest] + [least] * (count - 1), total - largest - least * (count - 1)
    while spare > 0:
        candidates = [i for i in range(1, count) if holding[i] < largest] or [i for i in range(1, count) if holding[i] < reach]
        mass, remaining = sum([portions[i] for i in candidates]), spare
        for i in candidates:
            addition = min(reach - holding[i], max(1, remaining * portions[i] // mass), spare)
            holding[i] = holding[i] + addition
            spare = spare - addition
    return np.array(holding)


def centred(rng, dims, deviation, bound, split=(), held_as=jnp.bfloat16):
    array = jax.random.normal(rng, dims, jnp.float32) * deviation
    if len(split) > 0:
        array = steps_of(rng, dims, split, -0.22, 0.18) * array
    return jnp.clip(array, min=-bound, max=bound).astype(held_as)


def setup_inputs(seed: int = 0) -> dict:
    seeds = jax.random.split(jax.random.key(seed), 10)
    transformed = centred(seeds[0], (NAUX, NT * TILE), 1.0, 6.0, ((0, 8), (1, 32)))
    coupling = centred(seeds[1], (NAUX, NAUX), NAUX ** -0.5, 0.09375, ((0, 8),))
    block_mask = touch_ends((jax.random.randint(seeds[2], (NAUX // ZBLK, NAUX // ZBLK), 0, 4) < 3).astype(jnp.int32), jax.random.fold_in(seeds[2], 1), 0, 1)
    density_row = centred(seeds[3], (NBLK * TILE, TILE), TILE ** -0.5, 0.5, ((0, 32),))
    density_col = centred(seeds[4], (NBLK * TILE, TILE), TILE ** -0.5, 0.5, ((0, 32),))
    row_owner_keys = jax.random.split(jax.random.fold_in(seeds[5], 1), NT // TILES_DEV)
    row_owner_turns = jax.random.permutation(jax.random.fold_in(seeds[5], 3), NT // TILES_DEV)
    row_owner = jax.vmap(lambda own, number: deal_out(jax.random.fold_in(seeds[5], 2), own, number, TILES_DEV, N_TILE, 1, CAP, 2))(row_owner_keys, row_owner_turns).reshape((NT, 1))
    row_slot = touch_ends(jax.random.randint(seeds[6], (NT, 1), 0, BLK_DEV), jax.random.fold_in(seeds[6], 1), 0, BLK_DEV - 1).astype(jnp.int32)
    col_owner_keys = jax.random.split(jax.random.fold_in(seeds[7], 1), NT // TILES_DEV)
    col_owner_turns = jax.random.permutation(jax.random.fold_in(seeds[7], 3), NT // TILES_DEV)
    col_owner = jax.vmap(lambda own, number: deal_out(jax.random.fold_in(seeds[7], 2), own, number, TILES_DEV, N_TILE, 1, CAP, 2))(col_owner_keys, col_owner_turns).reshape((NT, 1))
    col_slot = touch_ends(jax.random.randint(seeds[8], (NT, 1), 0, BLK_DEV), jax.random.fold_in(seeds[8], 1), 0, BLK_DEV - 1).astype(jnp.int32)
    return {"transformed": transformed, "coupling": coupling, "block_mask": block_mask, "density_row": density_row, "density_col": density_col, "row_owner": row_owner, "row_slot": row_slot, "col_owner": col_owner, "col_slot": col_slot}


def reference(transformed, coupling, block_mask, density_row, density_col, row_owner, row_slot, col_owner, col_slot):
    expanded = jnp.repeat(jnp.repeat(block_mask, ZBLK, axis=0), ZBLK, axis=1).astype(jnp.bfloat16)
    masked = coupling * expanded
    nblk = BLK_DEV * N_TILE
    pos_row = row_owner[:, 0] * BLK_DEV + row_slot[:, 0]
    pos_col = col_owner[:, 0] * BLK_DEV + col_slot[:, 0]
    blocks = jnp.arange(nblk, dtype=jnp.int32)
    hot_row = (pos_row[None, :] == blocks[:, None]).astype(jnp.float32)
    hot_col = (pos_col[None, :] == blocks[:, None]).astype(jnp.float32)

    def step(carry, group):
        start = (group * TILES_DEV * TILE).astype(jnp.int32)
        columns = lax.dynamic_slice_in_dim(transformed, start, TILES_DEV * TILE, 1)
        gtiles = jnp.dot(masked, columns, preferred_element_type=jnp.float32).astype(jnp.bfloat16)
        gtiles = gtiles.astype(jnp.float32).reshape(NAUX, TILES_DEV, TILE)
        first = (group * TILES_DEV).astype(jnp.int32)
        part_row = lax.dynamic_slice_in_dim(hot_row, first, TILES_DEV, 1)
        part_col = lax.dynamic_slice_in_dim(hot_col, first, TILES_DEV, 1)
        sum_row = carry[0] + jnp.einsum('bt,ptk->bpk', part_row, gtiles)
        sum_col = carry[1] + jnp.einsum('bt,ptk->bpk', part_col, gtiles)
        return (sum_row, sum_col), None

    empty = jnp.zeros((nblk, NAUX, TILE), jnp.float32)
    (sum_row, sum_col), _ = lax.scan(step, (empty, empty), jnp.arange(N_TILE, dtype=jnp.int32))
    sum_row = sum_row.astype(jnp.bfloat16).astype(jnp.float32)
    sum_col = sum_col.astype(jnp.bfloat16).astype(jnp.float32)
    dens_row = density_row.astype(jnp.float32).reshape(nblk, TILE, TILE)
    dens_col = density_col.astype(jnp.float32).reshape(nblk, TILE, TILE)
    grad_row = jnp.einsum('bph,bhk->pbk', sum_row, dens_row).reshape(NAUX, nblk * TILE)
    grad_col = jnp.einsum('bph,bhk->pbk', sum_col, dens_col).reshape(NAUX, nblk * TILE)
    return grad_row, grad_col
```

```python
import jax
import jax.numpy as jnp
from jax import lax
from jax.sharding import PartitionSpec as P


def shards(
    transformed,
    coupling,
    block_mask,
    density_row,
    density_col,
    row_owner,
    row_slot,
    col_owner,
    col_slot,
):
    aux_dev = coupling.shape[0]
    naux = coupling.shape[1]
    zblock = naux // block_mask.shape[0]
    n_tile = lax.axis_size("tile")
    me_aux = lax.axis_index("aux")
    me_tile = lax.axis_index("tile")
    mask_rows = lax.dynamic_slice_in_dim(
        block_mask, me_aux * (aux_dev // zblock), aux_dev // zblock, 0
    )
    expanded = jnp.repeat(jnp.repeat(mask_rows, zblock, axis=0), zblock, axis=1).astype(
        jnp.bfloat16
    )
    masked = coupling * expanded
    pairs = transformed.shape[1]
    gtiles = transformed
    width = density_row.shape[1]
    tiles_dev = pairs // width
    blk_dev = density_row.shape[0] // width
    capacity = max(2, 2 * tiles_dev // n_tile)
    three = gtiles.reshape(aux_dev, tiles_dev, width)
    first = me_tile * tiles_dev

    def pack(owner_list, slot_list):
        owners = lax.dynamic_slice_in_dim(owner_list[:, 0], first, tiles_dev, 0)
        slots = lax.dynamic_slice_in_dim(slot_list[:, 0], first, tiles_dev, 0)
        dest_hot = (owners[:, None] == jnp.arange(n_tile, dtype=jnp.int32)[None, :]).astype(
            jnp.int32
        )
        rank = jnp.sum(jnp.cumsum(dest_hot, axis=0) * dest_hot, axis=1) - 1
        target = owners * capacity + rank
        place = (target[None, :] == jnp.arange(n_tile * capacity, dtype=jnp.int32)[:, None]).astype(
            jnp.bfloat16
        )
        packed = jnp.einsum("st,ptk->spk", place, three, preferred_element_type=jnp.float32).astype(
            jnp.bfloat16
        )
        slot_hot = (slots[:, None] == jnp.arange(blk_dev, dtype=jnp.int32)[None, :]).astype(
            jnp.bfloat16
        )
        marks = jnp.dot(place, slot_hot, preferred_element_type=jnp.float32).astype(jnp.bfloat16)
        return (
            packed.reshape(n_tile, capacity, aux_dev, width),
            marks.reshape(n_tile, capacity, blk_dev),
        )

    send_row, mark_row = pack(row_owner, row_slot)
    send_col, mark_col = pack(col_owner, col_slot)
    recv_row, got_row, recv_col, got_col = (
        lax.all_to_all(send_row, "tile", split_axis=0, concat_axis=0, tiled=True),
        lax.all_to_all(mark_row, "tile", split_axis=0, concat_axis=0, tiled=True),
        lax.all_to_all(send_col, "tile", split_axis=0, concat_axis=0, tiled=True),
        lax.all_to_all(mark_col, "tile", split_axis=0, concat_axis=0, tiled=True),
    )

    def contract(received, marks, density):
        flat = received.reshape(n_tile * capacity, aux_dev, width)
        weights = marks.reshape(n_tile * capacity, blk_dev)
        sums = jnp.einsum(
            "sb,spk->pbk", weights, flat, preferred_element_type=jnp.float32
        ).astype(jnp.bfloat16)
        gathered = lax.all_gather(
            sums.reshape(aux_dev, blk_dev * width), "aux", axis=0, tiled=True
        )
        totals = jnp.dot(masked, gathered, preferred_element_type=jnp.float32)
        totals = totals.astype(jnp.bfloat16).reshape(aux_dev, blk_dev, width)
        dens = density.reshape(blk_dev, width, width)
        result = jnp.einsum("pbh,bhk->pbk", totals, dens, preferred_element_type=jnp.float32)
        return result.reshape(aux_dev, blk_dev * width)

    grad_row = contract(recv_row, got_row, density_row)
    grad_col = contract(recv_col, got_col, density_col)
    return (grad_row, grad_col)


def solution(mesh):
    placed = (
        P("aux", "tile"),
        P("aux", None),
        P(),
        P("tile", None),
        P("tile", None),
        P(),
        P(),
        P(),
        P(),
    )
    return jax.shard_map(
        shards,
        mesh=mesh,
        in_specs=placed,
        out_specs=(P("aux", "tile"), P("aux", "tile")),
        check_vma=False,
    )
```

```python
import functools

import jax
import jax.numpy as jnp
from jax import lax
from jax.experimental import pallas as pl
from jax.experimental.pallas import tpu as pltpu
from jax.sharding import PartitionSpec as P

RING = 4
CORES = 2
W = 128
CHUNKS = ((0, 0, 128), (1, 0, 128), (2, 0, 128), (3, 0, 128))
SUBS = 2
F32, BF16 = jnp.float32, jnp.bfloat16


def kernel(nz, tiles, tbl, mask, t_hbm, c_hbm, dr, dc, out_r, out_c, *scratch):
    n = len(CHUNKS)
    groups = c_hbm.shape[1] // (nz * W)
    it = iter(scratch)
    take = lambda k: [next(it) for _ in range(k)]
    raw, rest, sa, ra, sb, rb, us = (take(n) for _ in range(7))
    uz = take(groups)
    amat = take(groups)
    own, total = take(2)
    (a_sem, loc_sem, e1_send, sib_send, e1_recv, fw_send, ea_send, ea_recv, eb_send, eb_recv,
     es_send, es_recv, z_send, z_recv) = take(14)

    z, t = lax.axis_index("aux"), lax.axis_index("tile")
    c, x, y = t % CORES, (t // CORES) % RING, t // (CORES * RING)

    def tid(yy, xx, cc):
        return (yy * RING + xx) * CORES + cc

    def pick(for0, for1):
        return for0 + c * (for1 - for0)

    def first(d):
        return pick(tid(y, (x + RING + d) % RING, 0), tid((y + RING + d) % RING, x, 1))

    def crossed(d):
        return pick(tid((y + RING + d) % RING, x, 1), tid(y, (x + RING + d) % RING, 0))

    def second(d):
        return pick(tid((y + RING + d) % RING, x, 0), tid(y, (x + RING + d) % RING, 1))

    sibling = tid(y, x, 1 - c)
    m2 = pick(y, x)
    g_opp, g_p, g_m = (m2 + 2) % RING, (m2 + 1) % RING, (m2 + 3) % RING
    z_to = ((z + 1) % nz, (z + nz - 1) % nz)
    sent = []

    def remote(src, dst, send, recv, zz, tt):
        return pltpu.make_async_remote_copy(
            src_ref=src, dst_ref=dst, send_sem=send, recv_sem=recv,
            device_id=(zz, tt), device_id_type=pl.DeviceIdType.MESH)

    def go(src, dst, send, recv, zz, tt):
        copy = remote(src, dst, send, recv, zz, tt)
        copy.start()
        sent.append(copy)

    def arrived(ref, recv):
        remote(ref, ref, a_sem.at[0], recv, z, sibling).wait_recv()

    def rows_of(i, h):
        g, off, rows = CHUNKS[i]
        return pl.ds(pl.multiple_of(g * W + off + h * (rows // 2), 16), rows // 2)

    def slot(i, s):
        return raw[i].at[s, pl.ds(0, tiles)]

    def load_raw(i):
        for k, (h, to) in enumerate(((c, slot(i, c)), (1 - c, rest[i]))):
            def body(e, carry, h=h, to=to, k=k):
                pltpu.make_async_copy(
                    t_hbm.at[rows_of(i, h), pl.ds(pl.multiple_of(e * W, W), W)],
                    to.at[e], loc_sem.at[i, k]).start()
                return carry

            lax.fori_loop(0, tiles, body, 0)

    for i in range(n):
        load_raw(i)

    a_copies = []
    for g in range(groups):
        for b in range(nz):
            copy = pltpu.make_async_copy(
                c_hbm.at[:, pl.ds((b * groups + g) * W, W)],
                amat[g].at[:, pl.ds(b * W, W)], a_sem.at[g])
            copy.start()
            a_copies.append(copy)
    for i in range(n):
        for s in range(2 * RING):
            raw[i][s, tiles] = jnp.zeros(raw[i].shape[2:], BF16)

    barrier = pltpu.get_barrier_semaphore()
    near = [(z, sibling), (z_to[0], t), (z_to[1], t)]
    for d in (1, -1):
        for cc in range(CORES):
            near.append((z, tid(y, (x + RING + d) % RING, cc)))
            near.append((z, tid((y + RING + d) % RING, x, cc)))
    for who in near:
        pl.semaphore_signal(barrier, inc=1, device_id=who, device_id_type=pl.DeviceIdType.MESH)
    pl.semaphore_wait(barrier, len(near))

    def start_raw(i):
        for k, (src, to) in enumerate(((slot(i, c), first), (rest[i], crossed))):
            pltpu.make_async_copy(src, src, loc_sem.at[i, k]).wait()
            for m, d in enumerate((1, -1)):
                s = ((RING - d) % RING) * CORES + c
                go(src, slot(i, s), e1_send.at[i, 2 * k + m], e1_recv.at[i, s], z, to(d))
        go(rest[i], slot(i, c), sib_send.at[i], e1_recv.at[i, c], z, sibling)

    def forward_raw(i):
        for d, s in ((1, 6), (-1, 3)):
            arrived(slot(i, s), e1_recv.at[i, s])
            to = 2 * CORES + (0 if d == 1 else 1)
            go(slot(i, s), slot(i, to), fw_send.at[i, 0 if d == 1 else 1], e1_recv.at[i, to],
               z, first(d))

    def finish_raw(i):
        arrived(slot(i, 1 - c), e1_recv.at[i, 1 - c])
        for s in (2, 7, 4, 5):
            arrived(slot(i, s), e1_recv.at[i, s])

    def summed(i, g, j):
        acc = None
        for e in range(4 * RING):
            v = raw[i][e // 2, tbl[(g * 16 + j) * 16 + e]].astype(F32)
            acc = v if acc is None else acc + v
        return acc

    def fill(i, g, low, high, store, extra=None):
        def body(j, carry):
            v = summed(i, g, j)
            if extra is not None:
                v = v + extra[j - low].astype(F32)
            store[j] = v.astype(store.dtype)
            return carry

        lax.fori_loop(low, high, body, 0)

    def scatter_a(i):
        fill(i, g_opp, 0, 16, sa[i])
        go(sa[i].at[pl.ds(0, 8)], ra[i].at[0], ea_send.at[i, 0], ea_recv.at[i, 0], z, second(1))
        go(sa[i].at[pl.ds(8, 8)], ra[i].at[1], ea_send.at[i, 1], ea_recv.at[i, 1], z, second(-1))

    def scatter_b(i):
        fill(i, g_p, 8, 16, sb[i].at[0])
        fill(i, g_m, 0, 8, sb[i].at[1])
        arrived(ra[i].at[0], ea_recv.at[i, 0])
        fill(i, g_p, 0, 8, sb[i].at[0], ra[i].at[0])
        go(sb[i].at[0], rb[i].at[0], eb_send.at[i, 0], eb_recv.at[i, 0], z, second(1))
        arrived(ra[i].at[1], ea_recv.at[i, 1])
        fill(i, g_m, 8, 16, sb[i].at[1], ra[i].at[1])
        go(sb[i].at[1], rb[i].at[1], eb_send.at[i, 1], eb_recv.at[i, 1], z, second(-1))
        fill(i, m2, 0, 16, own)

    def part(i, zz, first_row, rows):
        g, off, _ = CHUNKS[i]
        return uz[g].at[zz, pl.ds(pl.multiple_of(off + first_row, 16), rows)]

    def owners(i):
        g, off, rows = CHUNKS[i]
        half = rows // 2
        mine = pl.ds(pl.multiple_of(off + c * half, 16), half)
        for k in range(2):
            arrived(rb[i].at[k], eb_recv.at[i, k])

        def position(j):
            return own[j] + rb[i][0, j].astype(F32) + rb[i][1, j].astype(F32)

        for jj in range(8):
            us[i][:, jj * W:(jj + 1) * W] = position((1 - c) * 8 + jj).astype(BF16)
        go(us[i], part(i, z, c * half, half), es_send.at[i], es_recv.at[i], z, sibling)
        for jj in range(8):
            uz[g][z, mine, jj * W:(jj + 1) * W] = position(c * 8 + jj).astype(BF16)

    def z_copy(i, k, step, q):
        rows = CHUNKS[i][2] // SUBS
        origin = (z + (nz - step if k == 0 else step)) % nz
        ref = part(i, origin, q * rows, rows)
        go(ref, ref, z_send.at[i, k, step * SUBS + q], z_recv.at[i, k, step * SUBS + q],
           z_to[k], t)

    def z_wait(i, k, step, q):
        rows = CHUNKS[i][2] // SUBS
        origin = (z + (2 * nz - 1 - step if k == 0 else step + 1)) % nz
        arrived(part(i, origin, q * rows, rows), z_recv.at[i, k, step * SUBS + q])

    def z_begin(i):
        half = CHUNKS[i][2] // 2
        arrived(part(i, z, (1 - c) * half, half), es_recv.at[i])
        for q in range(SUBS):
            for k in range(2):
                z_copy(i, k, 0, q)

    last = nz // 2 - 1

    def z_forward(i, step):
        for q in range(SUBS):
            for k in range(2):
                z_wait(i, k, step - 1, q)
                if step < last or (q * 2 // SUBS) == k:
                    z_copy(i, k, step, q)

    def z_end(i):
        for q in range(SUBS):
            z_wait(i, q * 2 // SUBS, last, q)

    def masked():
        for copy in a_copies:
            copy.wait()
        rows = amat[0].shape[0] // W
        for g in range(groups):
            def body(e, carry):
                b, p = e // rows, e % rows
                keep = mask[z * rows + p, b * groups + g].astype(F32)
                at = (pl.ds(pl.multiple_of(p * W, W), W), pl.ds(pl.multiple_of(b * W, W), W))
                amat[g][at] = (amat[g][at].astype(F32) * keep).astype(BF16)
                return carry

            lax.fori_loop(0, nz * rows, body, 0)

    step_n = 256

    def product(g):
        def body(e, carry):
            at = pl.ds(pl.multiple_of(e * step_n, step_n), step_n)
            right = uz[g][:, :, at].reshape(nz * W, step_n)
            new = jnp.dot(amat[g][...], right, preferred_element_type=F32)
            if g > 0:
                new = new + total[:, at]
            total[:, at] = new
            return carry

        lax.fori_loop(0, total.shape[1] // step_n, body, 0)

    def done_group(i):
        g, off, rows = CHUNKS[i]
        return g if off + rows == W else None

    start_raw(0)
    masked()
    forward_raw(0)
    finish_raw(0)
    if n > 1:
        start_raw(1)
    for i in range(n):
        scatter_a(i)
        if i > 0:
            z_forward(i - 1, 1)
        scatter_b(i)
        if i + 1 < n:
            forward_raw(i + 1)
        if i > 0:
            z_forward(i - 1, 2)
        owners(i)
        if i > 0:
            z_forward(i - 1, 3)
        z_begin(i)
        if i + 1 < n:
            finish_raw(i + 1)
        if i + 2 < n:
            start_raw(i + 2)
        if i > 0:
            z_end(i - 1)
            if done_group(i - 1) is not None:
                product(done_group(i - 1))
    for s in (1, 2, 3):
        z_forward(n - 1, s)
    z_end(n - 1)
    product(done_group(n - 1))

    blocks = dr.shape[0] // W
    for k, (dens, out) in enumerate(((dr, out_r), (dc, out_c))):
        for b in range(blocks):
            at = (k * blocks + b) * W
            s = total[:, at:at + W]
            high = s.astype(BF16)
            low = (s - high.astype(F32)).astype(BF16)
            d = dens[b * W:(b + 1) * W, :]
            out[:, b * W:(b + 1) * W] = jnp.dot(high, d, preferred_element_type=F32) + jnp.dot(
                low, d, preferred_element_type=F32)
    for copy in sent:
        copy.wait_send()


def tables(row_owner, row_slot, col_owner, col_slot, slots):
    t = lax.axis_index("tile")
    c, x, y = t % CORES, (t // CORES) % RING, t // (CORES * RING)
    tiles = row_owner.shape[0] // (RING * RING * CORES)
    key = jnp.stack([(row_owner * slots + row_slot)[:, 0], (col_owner * slots + col_slot)[:, 0]])
    key = key.reshape(2, RING, RING, CORES, tiles)
    key = jnp.where(c == 0, lax.dynamic_index_in_dim(key, y, 1, False),
                    lax.dynamic_index_in_dim(key, x, 2, False))
    mine = jnp.where(c == 0, x, y)
    key = lax.dynamic_slice_in_dim(jnp.concatenate([key, key], 1), mine, RING, 1)
    k = jnp.arange(tiles, dtype=jnp.int32)
    earlier = (key[..., None, :] == key[..., :, None]) & (k[None, :] < k[:, None])
    rank = jnp.sum(earlier.astype(jnp.int32), axis=-1)
    g = jnp.arange(RING, dtype=jnp.int32)
    base = jnp.where(c == 0, (g * RING + x) * CORES, (y * RING + g) * CORES)
    want = (base[:, None] + jnp.arange(CORES, dtype=jnp.int32)[None, :])[:, :, None] * slots
    want = want + jnp.arange(slots, dtype=jnp.int32)[None, None, :]
    want = want[:, :, None, :, None, None, None, None]
    hit = (key[None, None, :, None, :, :, None, :] == want) & (
        rank[None, None, :, None, :, :, None, :]
        == jnp.arange(2, dtype=jnp.int32)[None, None, None, None, None, None, :, None])
    spot = jnp.min(jnp.where(hit, k, tiles), axis=-1)
    return spot.reshape(-1)


def shards(transformed, coupling, block_mask, density_row, density_col,
           row_owner, row_slot, col_owner, col_slot):
    nz = lax.axis_size("aux")
    aux_dev, pairs = transformed.shape
    tiles = pairs // W
    slots = density_row.shape[0] // W
    columns = 2 * density_row.shape[0]
    groups = aux_dev // W
    tbl = tables(row_owner, row_slot, col_owner, col_slot, slots)
    n = len(CHUNKS)
    halves = [c[2] // 2 for c in CHUNKS]
    scratch = []
    scratch += [pltpu.VMEM((2 * RING, tiles + 1, h, W), BF16) for h in halves]
    scratch += [pltpu.VMEM((tiles, h, W), BF16) for h in halves]
    scratch += [pltpu.VMEM((16, h, W), BF16) for h in halves]
    scratch += [pltpu.VMEM((2, 8, h, W), BF16) for h in halves]
    scratch += [pltpu.VMEM((2, 16, h, W), BF16) for h in halves]
    scratch += [pltpu.VMEM((2, 16, h, W), BF16) for h in halves]
    scratch += [pltpu.VMEM((h, columns), BF16) for h in halves]
    scratch += [pltpu.VMEM((nz, W, columns), BF16) for _ in range(groups)]
    scratch += [pltpu.VMEM((aux_dev, nz * W), BF16) for _ in range(groups)]
    scratch += [pltpu.VMEM((16, max(halves), W), F32), pltpu.VMEM((aux_dev, columns), F32)]
    dma = pltpu.SemaphoreType.DMA
    steps = nz // 2 * SUBS
    scratch += [dma((groups,)), dma((n, 2)), dma((n, 4)), dma((n,)), dma((n, 8)), dma((n, 2)),
                dma((n, 2)), dma((n, 2)), dma((n, 2)), dma((n, 2)), dma((n,)), dma((n,)),
                dma((n, 2, steps)), dma((n, 2, steps))]
    vmem, smem = pl.BlockSpec(memory_space=pltpu.VMEM), pl.BlockSpec(memory_space=pltpu.SMEM)
    hbm = pl.BlockSpec(memory_space=pl.ANY)
    shape = jax.ShapeDtypeStruct((aux_dev, columns // 2), F32)
    return pl.pallas_call(
        functools.partial(kernel, nz, tiles),
        out_shape=(shape, shape),
        in_specs=[smem, smem, hbm, hbm, vmem, vmem],
        out_specs=(vmem, vmem),
        scratch_shapes=scratch,
        compiler_params=pltpu.CompilerParams(
            collective_id=0, has_side_effects=True, vmem_limit_bytes=56 * 1024 * 1024),
        cost_estimate=pl.CostEstimate(
            flops=2 * aux_dev * nz * aux_dev * columns, bytes_accessed=16 << 20,
            transcendentals=0),
    )(tbl, block_mask, transformed, coupling, density_row, density_col)


def solution(mesh):
    placed = (P("aux", "tile"), P("aux", None), P(), P("tile", None), P("tile", None),
              P(), P(), P(), P())
    return jax.shard_map(shards, mesh=mesh, in_specs=placed,
                         out_specs=(P("aux", "tile"), P("aux", "tile")), check_vma=False)
```

```python
import functools

import jax
import jax.numpy as jnp
from jax import lax
from jax.experimental import pallas as pl
from jax.experimental.pallas import tpu as pltpu
from jax.sharding import PartitionSpec as P

RING = 4
CORES = 2
W = 128
CHUNKS = tuple((g, off, 64) for g in range(4) for off in (0, 64))
F32, BF16 = jnp.float32, jnp.bfloat16


def kernel(nz, tiles, slots, keys, mask, t_hbm, c_hbm, dr, dc, out_r, out_c, *scratch):
    n = len(CHUNKS)
    groups = c_hbm.shape[1] // (nz * W)
    it = iter(scratch)
    take = lambda k: [next(it) for _ in range(k)]
    raw, sa, ra, sb, rb, us = (take(n) for _ in range(6))
    uz = take(groups)
    amat = take(groups)
    tv, own, total, tbl_v, tbl = take(5)
    (a_sem, tv_sem, loc_sem, e1_send, sib_send, e1_recv, fw_send, ea_send, ea_recv, eb_send, eb_recv,
     es_send, es_recv, z_send, z_recv, tbl_sem) = take(16)

    z, t = lax.axis_index("aux"), lax.axis_index("tile")
    c, x, y = t % CORES, (t // CORES) % RING, t // (CORES * RING)

    def tid(yy, xx, cc):
        return (yy * RING + xx) * CORES + cc

    def pick(for0, for1):
        return for0 + c * (for1 - for0)

    def first(d):
        return pick(tid(y, (x + RING + d) % RING, 0), tid((y + RING + d) % RING, x, 1))

    def second(d):
        return pick(tid((y + RING + d) % RING, x, 0), tid(y, (x + RING + d) % RING, 1))

    sibling = tid(y, x, 1 - c)
    m1, m2 = pick(x, y), pick(y, x)
    g_opp, g_p, g_m = (m2 + 2) % RING, (m2 + 1) % RING, (m2 + 3) % RING
    z_to = ((z + 1) % nz, (z + nz - 1) % nz)
    sent = []

    def remote(src, dst, send, recv, zz, tt):
        return pltpu.make_async_remote_copy(
            src_ref=src, dst_ref=dst, send_sem=send, recv_sem=recv,
            device_id=(zz, tt), device_id_type=pl.DeviceIdType.MESH)

    def go(src, dst, send, recv, zz, tt):
        copy = remote(src, dst, send, recv, zz, tt)
        copy.start()
        sent.append(copy)

    def arrived(ref, recv):
        remote(ref, ref, a_sem.at[0], recv, z, sibling).wait_recv()

    def rows_of(i, h):
        g, off, rows = CHUNKS[i]
        return pl.ds(pl.multiple_of(g * W + off + h * (rows // 2), 16), rows // 2)

    def slot(i, s):
        return raw[i].at[s, pl.ds(0, tiles)]

    head = CHUNKS[0][2]
    spans = (pl.ds(0, head), pl.ds(head, tv.shape[1] - head))

    def load_tiles(k):
        def body(e, carry):
            pltpu.make_async_copy(
                t_hbm.at[spans[k], pl.ds(pl.multiple_of(e * W, W), W)],
                tv.at[e, spans[k]], tv_sem.at[k]).start()
            return carry

        lax.fori_loop(0, tiles, body, 0)

    def loaded(k):
        span = tv.at[:, spans[k]]
        pltpu.make_async_copy(span, span, tv_sem.at[k]).wait()

    a_copies = []

    def load_coupling():
        for g in range(groups):
            for b in range(nz):
                copy = pltpu.make_async_copy(
                    c_hbm.at[:, pl.ds((b * groups + g) * W, W)],
                    amat[g].at[:, pl.ds(b * W, W)], a_sem.at[g])
                copy.start()
                a_copies.append(copy)

    def empty_tiles(i):
        for s in range(2 * RING):
            raw[i][s, tiles] = jnp.zeros(raw[i].shape[2:], BF16)

    def build_table():
        half = 2 * RING * slots
        row = lax.broadcasted_iota(jnp.int32, (half, 1), 0)
        gg, co, sl = row // (CORES * slots), row // slots % CORES, row % slots
        want = pick((gg * RING + x) * CORES + co, (y * RING + gg) * CORES + co) * slots + sl
        lane = lax.broadcasted_iota(jnp.int32, (half, keys.shape[1]), 1)
        entry = lax.broadcasted_iota(jnp.int32, (half, W), 1)
        for side in range(2):
            hit = keys[side:side + 1, :] == want
            table = jnp.zeros((half, W), jnp.int32)
            for s in range(2 * RING):
                a = (m1 + s // CORES) % RING
                low = tid(pick(y, a), pick(a, x), s % CORES) * tiles
                here = hit & (lane >= low) & (lane < low + tiles)
                least = jnp.min(jnp.where(here, lane, 1 << 20), axis=1, keepdims=True)
                most = jnp.max(jnp.where(here, lane, -1), axis=1, keepdims=True)
                k0 = jnp.where(most >= 0, least - low, tiles)
                k1 = jnp.where(most > least, most - low, tiles)
                table = jnp.where(entry == 2 * s, k0, jnp.where(entry == 2 * s + 1, k1, table))
            tbl_v[side * half:(side + 1) * half, :] = table
        copy = pltpu.make_async_copy(tbl_v, tbl, tbl_sem.at[0])
        copy.start()
        copy.wait()

    barrier = pltpu.get_barrier_semaphore()
    near = [(z, sibling), (z_to[0], t), (z_to[1], t)]
    for d in (1, -1):
        near.append((z, first(d)))
        near.append((z, second(d)))
    for who in near:
        pl.semaphore_signal(barrier, inc=1, device_id=who, device_id_type=pl.DeviceIdType.MESH)
    load_tiles(0)
    empty_tiles(0)
    pl.semaphore_wait(barrier, len(near))

    def local(i):
        return pltpu.make_async_copy(tv.at[:, rows_of(i, c)], slot(i, c), loc_sem.at[i])

    def to_sibling(i):
        go(tv.at[:, rows_of(i, 1 - c)], slot(i, c), sib_send.at[i], e1_recv.at[i, c], z, sibling)
        local(i).start()

    def start_own(i):
        send_raw(i, 0, c, tv.at[:, rows_of(i, c)])

    def start_sib(i):
        arrived(slot(i, 1 - c), e1_recv.at[i, 1 - c])
        send_raw(i, 1, 1 - c, slot(i, 1 - c))

    def send_raw(i, k, cc, src):
        for m, d in enumerate((1, -1)):
            s = ((RING - d) % RING) * CORES + cc
            go(src, slot(i, s), e1_send.at[i, 2 * k + m], e1_recv.at[i, s], z, first(d))

    def start_raw(i):
        start_own(i)
        start_sib(i)

    def forward_raw(i):
        for m, (d, s, cc) in enumerate(((1, 6 + c, c), (-1, 2 + 1 - c, 1 - c))):
            arrived(slot(i, s), e1_recv.at[i, s])
            go(slot(i, s), slot(i, 4 + cc), fw_send.at[i, m], e1_recv.at[i, 4 + cc], z, first(d))

    def finish_raw(i):
        local(i).wait()
        for s in (6 + 1 - c, 2 + c, 4, 5):
            arrived(slot(i, s), e1_recv.at[i, s])

    def summed(i, g, j):
        acc = None
        row = (j // slots % 2) * (2 * RING * slots) + (g * CORES + j // (2 * slots)) * slots + j % slots
        for e in range(4 * RING):
            v = raw[i][e // 2, tbl[row, e]].astype(F32)
            acc = v if acc is None else acc + v
        return acc

    def fill(i, g, low, high, store, extra=None):
        def body(j, carry):
            v = summed(i, g, j)
            if extra is not None:
                v = v + extra[j - low].astype(F32)
            store[j] = v.astype(store.dtype)
            return carry

        lax.fori_loop(low, high, body, 0)

    def scatter_a(i):
        fill(i, g_opp, 0, 16, sa[i])
        go(sa[i].at[pl.ds(0, 8)], ra[i].at[0], ea_send.at[i, 0], ea_recv.at[i, 0], z, second(1))
        go(sa[i].at[pl.ds(8, 8)], ra[i].at[1], ea_send.at[i, 1], ea_recv.at[i, 1], z, second(-1))

    def scatter_b(i):
        fill(i, g_p, 8, 16, sb[i].at[0])
        fill(i, g_m, 0, 8, sb[i].at[1])
        arrived(ra[i].at[0], ea_recv.at[i, 0])
        fill(i, g_p, 0, 8, sb[i].at[0], ra[i].at[0])
        go(sb[i].at[0], rb[i].at[0], eb_send.at[i, 0], eb_recv.at[i, 0], z, second(1))
        arrived(ra[i].at[1], ea_recv.at[i, 1])
        fill(i, g_m, 8, 16, sb[i].at[1], ra[i].at[1])
        go(sb[i].at[1], rb[i].at[1], eb_send.at[i, 1], eb_recv.at[i, 1], z, second(-1))
        fill(i, m2, 0, 16, own.at[:, pl.ds(0, CHUNKS[i][2] // 2)])

    def part(i, zz, first_row, rows):
        g, off, _ = CHUNKS[i]
        return uz[g].at[zz, pl.ds(pl.multiple_of(off + first_row, 16), rows)]

    def owners(i):
        g, off, rows = CHUNKS[i]
        half = rows // 2
        mine = pl.ds(pl.multiple_of(off + c * half, 16), half)
        for k in range(2):
            arrived(rb[i].at[k], eb_recv.at[i, k])

        def position(j):
            return own[j, :half] + rb[i][0, j].astype(F32) + rb[i][1, j].astype(F32)

        for jj in range(8):
            us[i][:, jj * W:(jj + 1) * W] = position((1 - c) * 8 + jj).astype(BF16)
        go(us[i], part(i, z, c * half, half), es_send.at[i], es_recv.at[i], z, sibling)
        for jj in range(8):
            uz[g][z, mine, jj * W:(jj + 1) * W] = position(c * 8 + jj).astype(BF16)

    last = nz // 2 - 1

    def z_part(i, k, step, origin):
        rows = CHUNKS[i][2]
        if step == last:
            return part(i, origin, k * (rows // 2), rows // 2)
        return part(i, origin, 0, rows)

    def z_copy(i, k, step):
        ref = z_part(i, k, step, (z + (nz - step if k == 0 else step)) % nz)
        go(ref, ref, z_send.at[i, k, step], z_recv.at[i, k, step], z_to[k], t)

    def z_wait(i, k, step):
        origin = (z + (2 * nz - 1 - step if k == 0 else step + 1)) % nz
        arrived(z_part(i, k, step, origin), z_recv.at[i, k, step])

    def z_begin(i):
        half = CHUNKS[i][2] // 2
        arrived(part(i, z, (1 - c) * half, half), es_recv.at[i])
        for k in range(2):
            z_copy(i, k, 0)

    def z_forward(i, step):
        for k in range(2):
            z_wait(i, k, step - 1)
            z_copy(i, k, step)

    def z_end(i):
        for k in range(2):
            z_wait(i, k, last)

    def masked():
        for copy in a_copies:
            copy.wait()
        rows = amat[0].shape[0] // W
        for g in range(groups):
            def body(e, carry):
                b, p = e // rows, e % rows
                keep = mask[z * rows + p, b * groups + g].astype(F32)
                at = (pl.ds(pl.multiple_of(p * W, W), W), pl.ds(pl.multiple_of(b * W, W), W))
                amat[g][at] = (amat[g][at].astype(F32) * keep).astype(BF16)
                return carry

            lax.fori_loop(0, nz * rows, body, 0)

    step_n = 256

    def product(g):
        def body(e, carry):
            at = pl.ds(pl.multiple_of(e * step_n, step_n), step_n)
            right = uz[g][:, :, at].reshape(nz * W, step_n)
            new = jnp.dot(amat[g][...], right, preferred_element_type=F32)
            if g > 0:
                new = new + total[:, at]
            total[:, at] = new
            return carry

        lax.fori_loop(0, total.shape[1] // step_n, body, 0)

    def done_group(i):
        g, off, rows = CHUNKS[i]
        return g if off + rows == W else None

    def ring_end(i):
        z_end(i)
        if done_group(i) is not None:
            product(done_group(i))

    def ring_end(i):
        z_end(i)
        if done_group(i) is not None:
            product(done_group(i))

    loaded(0)
    to_sibling(0)
    start_own(0)
    load_tiles(1)
    start_sib(0)
    load_coupling()
    build_table()
    loaded(1)
    for i in range(1, n):
        to_sibling(i)
    forward_raw(0)
    for i in range(1, min(n, 3)):
        start_raw(i)
    for i in range(1, n):
        empty_tiles(i)
    for k in range(-2, n + 2):
        if k > -2:
            if k + 3 < n:
                forward_raw(k + 3)
            if k + 5 < n:
                start_raw(k + 5)
        if k + 2 < n:
            finish_raw(k + 2)
            scatter_a(k + 2)
        if k == -2:
            if n > 1:
                forward_raw(1)
            if n > 3:
                start_raw(3)
        if 0 <= k + 1 < n:
            owners(k + 1)
        if 0 <= k - 2 < n:
            ring_end(k - 2)
        if 0 <= k + 1 < n:
            z_begin(k + 1)
        if 0 <= k < n:
            z_forward(k, 2)
        if k + 2 < n:
            scatter_b(k + 2)
        if k == -1:
            masked()
        if 0 <= k + 1 < n:
            z_forward(k + 1, 1)
        if 0 <= k < n:
            z_forward(k, 3)

    blocks = dr.shape[0] // W
    for k, (dens, out) in enumerate(((dr, out_r), (dc, out_c))):
        for b in range(blocks):
            at = (k * blocks + b) * W
            s = total[:, at:at + W]
            high = s.astype(BF16)
            low = (s - high.astype(F32)).astype(BF16)
            d = dens[b * W:(b + 1) * W, :]
            out[:, b * W:(b + 1) * W] = jnp.dot(high, d, preferred_element_type=F32) + jnp.dot(
                low, d, preferred_element_type=F32)
    for copy in sent:
        copy.wait_send()


def shards(transformed, coupling, block_mask, density_row, density_col,
           row_owner, row_slot, col_owner, col_slot):
    nz = lax.axis_size("aux")
    aux_dev, pairs = transformed.shape
    tiles = pairs // W
    slots = density_row.shape[0] // W
    columns = 2 * density_row.shape[0]
    groups = aux_dev // W
    keys = jnp.stack([(row_owner * slots + row_slot)[:, 0], (col_owner * slots + col_slot)[:, 0]])
    keys = jnp.pad(keys, ((0, 0), (0, -keys.shape[1] % W)), constant_values=-1)
    n = len(CHUNKS)
    halves = [c[2] // 2 for c in CHUNKS]
    scratch = []
    scratch += [pltpu.VMEM((2 * RING, tiles + 1, h, W), BF16) for h in halves]
    scratch += [pltpu.VMEM((16, h, W), BF16) for h in halves]
    scratch += [pltpu.VMEM((2, 8, h, W), BF16) for h in halves]
    scratch += [pltpu.VMEM((2, 16, h, W), BF16) for h in halves]
    scratch += [pltpu.VMEM((2, 16, h, W), BF16) for h in halves]
    scratch += [pltpu.VMEM((h, columns), BF16) for h in halves]
    scratch += [pltpu.VMEM((nz, W, columns), BF16) for _ in range(groups)]
    scratch += [pltpu.VMEM((aux_dev, nz * W), BF16) for _ in range(groups)]
    scratch += [pltpu.VMEM((tiles, aux_dev, W), BF16)]
    scratch += [pltpu.VMEM((16, max(halves), W), F32), pltpu.VMEM((aux_dev, columns), F32),
                pltpu.VMEM((4 * RING * slots, W), jnp.int32),
                pltpu.SMEM((4 * RING * slots, W), jnp.int32)]
    dma = pltpu.SemaphoreType.DMA
    steps = nz // 2
    scratch += [dma((groups,)), dma((2,)), dma((n,)), dma((n, 4)), dma((n,)), dma((n, 8)), dma((n, 2)),
                dma((n, 2)), dma((n, 2)), dma((n, 2)), dma((n, 2)), dma((n,)), dma((n,)),
                dma((n, 2, steps)), dma((n, 2, steps)), dma((1,))]
    vmem, smem = pl.BlockSpec(memory_space=pltpu.VMEM), pl.BlockSpec(memory_space=pltpu.SMEM)
    hbm = pl.BlockSpec(memory_space=pl.ANY)
    shape = jax.ShapeDtypeStruct((aux_dev, columns // 2), F32)
    return pl.pallas_call(
        functools.partial(kernel, nz, tiles, slots),
        out_shape=(shape, shape),
        in_specs=[vmem, smem, hbm, hbm, vmem, vmem],
        out_specs=(vmem, vmem),
        scratch_shapes=scratch,
        compiler_params=pltpu.CompilerParams(
            collective_id=0, has_side_effects=True, vmem_limit_bytes=56 * 1024 * 1024),
        cost_estimate=pl.CostEstimate(
            flops=2 * aux_dev * nz * aux_dev * columns, bytes_accessed=16 << 20,
            transcendentals=0),
    )(keys, block_mask, transformed, coupling, density_row, density_col)


def solution(mesh):
    placed = (P("aux", "tile"), P("aux", None), P(), P("tile", None), P("tile", None),
              P(), P(), P(), P())
    return jax.shard_map(shards, mesh=mesh, in_specs=placed,
                         out_specs=(P("aux", "tile"), P("aux", "tile")), check_vma=False)
```

```python
import functools

import jax
import jax.numpy as jnp
from jax import lax
from jax.experimental import pallas as pl
from jax.experimental.pallas import tpu as pltpu
from jax.sharding import PartitionSpec as P

RING = 4
CORES = 2
W = 128
CHUNKS = ((0, 0, 32), (0, 32, 32), (0, 64, 64)) + tuple((g, off, 64) for g in (1, 2, 3) for off in (0, 64))
F32, BF16 = jnp.float32, jnp.bfloat16


def kernel(nz, tiles, slots, keys, mask, t_hbm, c_hbm, total, *scratch):
    n = len(CHUNKS)
    groups = c_hbm.shape[1] // (nz * W)
    it = iter(scratch)
    take = lambda k: [next(it) for _ in range(k)]
    raw, pb, rp, sa, ra, sb, rb, us = (take(n) for _ in range(8))
    uz = take(groups)
    amat = take(groups)
    tv, own, tbl_v, tbl = take(4)
    (a_sem, tv_sem, loc_sem, e1_send, sib_send, e1_recv, pb_send, pb_recv, ea_send, ea_recv, eb_send, eb_recv,
     es_send, es_recv, z_send, z_recv, tbl_sem) = take(17)

    z, t = lax.axis_index("aux"), lax.axis_index("tile")
    c, x, y = t % CORES, (t // CORES) % RING, t // (CORES * RING)

    def tid(yy, xx, cc):
        return (yy * RING + xx) * CORES + cc

    def pick(for0, for1):
        return for0 + c * (for1 - for0)

    def first(at):
        return pick(tid(y, at, 0), tid(at, x, 1))

    def second(d):
        return pick(tid((y + RING + d) % RING, x, 0), tid(y, (x + RING + d) % RING, 1))

    sibling = tid(y, x, 1 - c)
    m1, m2 = pick(x, y), pick(y, x)
    pair, across = m1 + 1 - 2 * (m1 % 2), RING - 1 - m1
    g_opp, g_p, g_m = (m2 + 2) % RING, (m2 + 1) % RING, (m2 + 3) % RING
    order = (g_opp, g_p, g_m, m2)
    z_to = ((z + 1) % nz, (z + nz - 1) % nz)
    sent = []

    def remote(src, dst, send, recv, zz, tt):
        return pltpu.make_async_remote_copy(
            src_ref=src, dst_ref=dst, send_sem=send, recv_sem=recv,
            device_id=(zz, tt), device_id_type=pl.DeviceIdType.MESH)

    def go(src, dst, send, recv, zz, tt):
        copy = remote(src, dst, send, recv, zz, tt)
        copy.start()
        sent.append(copy)

    def arrived(ref, recv):
        remote(ref, ref, a_sem.at[0], recv, z, sibling).wait_recv()

    def rows_of(i, h):
        g, off, rows = CHUNKS[i]
        return pl.ds(pl.multiple_of(g * W + off + h * (rows // 2), 16), rows // 2)

    def slot(i, s):
        return raw[i].at[s, pl.ds(0, tiles)]

    head = CHUNKS[0][2]
    spans = (pl.ds(0, head), pl.ds(head, tv.shape[1] - head))

    def load_tiles(k):
        def body(e, carry):
            pltpu.make_async_copy(
                t_hbm.at[spans[k], pl.ds(pl.multiple_of(e * W, W), W)],
                tv.at[e, spans[k]], tv_sem.at[k]).start()
            return carry

        lax.fori_loop(0, tiles, body, 0)

    def loaded(k):
        span = tv.at[:, spans[k]]
        pltpu.make_async_copy(span, span, tv_sem.at[k]).wait()

    a_copies = []

    def load_coupling():
        for g in range(groups):
            for b in range(nz):
                copy = pltpu.make_async_copy(
                    c_hbm.at[:, pl.ds((b * groups + g) * W, W)],
                    amat[g].at[:, pl.ds(b * W, W)], a_sem.at[g])
                copy.start()
                a_copies.append(copy)

    def empty_tiles(i):
        for s in range(2 * CORES):
            raw[i][s, tiles] = jnp.zeros(raw[i].shape[2:], BF16)

    def build_table():
        half = 2 * RING * slots
        row = lax.broadcasted_iota(jnp.int32, (half, 1), 0)
        gg, co, sl = row // (CORES * slots), row // slots % CORES, row % slots
        lane = lax.broadcasted_iota(jnp.int32, (half, keys.shape[1]), 1)
        entry = lax.broadcasted_iota(jnp.int32, (half, W), 1)
        for block in range(4):
            at, side = (m1, across)[block // 2], block % 2
            want = pick((gg * RING + at) * CORES + co, (at * RING + gg) * CORES + co) * slots + sl
            hit = keys[side:side + 1, :] == want
            table = jnp.zeros((half, W), jnp.int32)
            for s in range(2 * CORES):
                a = (m1, pair)[s // CORES]
                low = tid(pick(y, a), pick(a, x), s % CORES) * tiles
                here = hit & (lane >= low) & (lane < low + tiles)
                least = jnp.min(jnp.where(here, lane, 1 << 20), axis=1, keepdims=True)
                most = jnp.max(jnp.where(here, lane, -1), axis=1, keepdims=True)
                k0 = jnp.where(most >= 0, least - low, tiles)
                k1 = jnp.where(most > least, most - low, tiles)
                table = jnp.where(entry == 2 * s, k0, jnp.where(entry == 2 * s + 1, k1, table))
            tbl_v[block * half:(block + 1) * half, :] = table
        copy = pltpu.make_async_copy(tbl_v, tbl, tbl_sem.at[0])
        copy.start()
        copy.wait()

    barrier = pltpu.get_barrier_semaphore()
    near = [(z, sibling), (z_to[0], t), (z_to[1], t)]
    near += [(z, first(pair)), (z, first(across)), (z, second(1)), (z, second(-1))]
    for who in near:
        pl.semaphore_signal(barrier, inc=1, device_id=who, device_id_type=pl.DeviceIdType.MESH)
    load_tiles(0)
    build_table()
    load_tiles(1)
    for i in range(n):
        empty_tiles(i)
    loaded(0)
    pl.semaphore_wait(barrier, len(near))

    def local(i):
        return pltpu.make_async_copy(tv.at[:, rows_of(i, c)], slot(i, c), loc_sem.at[i])

    def to_sibling(i):
        go(tv.at[:, rows_of(i, 1 - c)], slot(i, c), sib_send.at[i], e1_recv.at[i, c], z, sibling)
        local(i).start()

    def start_own(i):
        send_raw(i, 0, c, tv.at[:, rows_of(i, c)])

    def start_sib(i):
        arrived(slot(i, 1 - c), e1_recv.at[i, 1 - c])
        send_raw(i, 1, 1 - c, slot(i, 1 - c))

    def send_raw(i, k, cc, src):
        to = CORES + cc
        go(src, slot(i, to), e1_send.at[i, k], e1_recv.at[i, to], z, first(pair))

    def start_raw(i):
        start_own(i)
        start_sib(i)

    def finish_raw(i):
        local(i).wait()
        for s in (2, 3):
            arrived(slot(i, s), e1_recv.at[i, s])

    def scatter_pair(i):
        for k, (low, high) in enumerate(((0, 1), (1, RING))):
            for r in range(low, high):
                fill(i, 1, order[r], 0, 16, pb[i].at[r])
            span = pl.ds(low, high - low)
            go(pb[i].at[span], rp[i].at[span], pb_send.at[i, k], pb_recv.at[i, k], z, first(across))

    def arrived_pair(i, k):
        arrived(rp[i].at[pl.ds(0, 1) if k == 0 else pl.ds(1, RING - 1)], pb_recv.at[i, k])

    def summed(i, w, g, j):
        acc = None
        row = ((w * 2 + j // slots % 2) * (2 * RING * slots)
               + (g * CORES + j // (2 * slots)) * slots + j % slots)
        for e in range(4 * CORES):
            v = raw[i][e // 2, tbl[row, e]].astype(F32)
            acc = v if acc is None else acc + v
        return acc

    def fill(i, w, g, low, high, store, *extras):
        def body(j, carry):
            v = summed(i, w, g, j)
            for ref, start in extras:
                v = v + ref[j - start].astype(F32)
            store[j] = v.astype(store.dtype)
            return carry

        lax.fori_loop(low, high, body, 0)

    def scatter_a(i):
        arrived_pair(i, 0)
        fill(i, 0, g_opp, 0, 16, sa[i], (rp[i].at[0], 0))
        go(sa[i].at[pl.ds(0, 8)], ra[i].at[0], ea_send.at[i, 0], ea_recv.at[i, 0], z, second(1))
        go(sa[i].at[pl.ds(8, 8)], ra[i].at[1], ea_send.at[i, 1], ea_recv.at[i, 1], z, second(-1))

    def scatter_b(i):
        arrived_pair(i, 1)
        fill(i, 0, g_p, 8, 16, sb[i].at[0], (rp[i].at[1], 0))
        fill(i, 0, g_m, 0, 8, sb[i].at[1], (rp[i].at[2], 0))
        arrived(ra[i].at[0], ea_recv.at[i, 0])
        fill(i, 0, g_p, 0, 8, sb[i].at[0], (rp[i].at[1], 0), (ra[i].at[0], 0))
        go(sb[i].at[0], rb[i].at[0], eb_send.at[i, 0], eb_recv.at[i, 0], z, second(1))
        arrived(ra[i].at[1], ea_recv.at[i, 1])
        fill(i, 0, g_m, 8, 16, sb[i].at[1], (rp[i].at[2], 0), (ra[i].at[1], 8))
        go(sb[i].at[1], rb[i].at[1], eb_send.at[i, 1], eb_recv.at[i, 1], z, second(-1))
        fill(i, 0, m2, 0, 16, own.at[:, pl.ds(0, CHUNKS[i][2] // 2)], (rp[i].at[3], 0))

    def part(i, zz, first_row, rows):
        g, off, _ = CHUNKS[i]
        return uz[g].at[zz, pl.ds(pl.multiple_of(off + first_row, 16), rows)]

    def owners(i):
        g, off, rows = CHUNKS[i]
        half = rows // 2
        mine = pl.ds(pl.multiple_of(off + c * half, 16), half)
        for k in range(2):
            arrived(rb[i].at[k], eb_recv.at[i, k])

        def position(j):
            return own[j, :half] + rb[i][0, j].astype(F32) + rb[i][1, j].astype(F32)

        for jj in range(8):
            us[i][:, jj * W:(jj + 1) * W] = position((1 - c) * 8 + jj).astype(BF16)
        go(us[i], part(i, z, c * half, half), es_send.at[i], es_recv.at[i], z, sibling)
        for jj in range(8):
            uz[g][z, mine, jj * W:(jj + 1) * W] = position(c * 8 + jj).astype(BF16)

    last = nz // 2 - 1

    def z_part(i, k, step, origin):
        rows = CHUNKS[i][2]
        if step == last:
            return part(i, origin, k * (rows // 2), rows // 2)
        return part(i, origin, 0, rows)

    def z_copy(i, k, step):
        ref = z_part(i, k, step, (z + (nz - step if k == 0 else step)) % nz)
        go(ref, ref, z_send.at[i, k, step], z_recv.at[i, k, step], z_to[k], t)

    def z_wait(i, k, step):
        origin = (z + (2 * nz - 1 - step if k == 0 else step + 1)) % nz
        arrived(z_part(i, k, step, origin), z_recv.at[i, k, step])

    def z_begin(i):
        half = CHUNKS[i][2] // 2
        arrived(part(i, z, (1 - c) * half, half), es_recv.at[i])
        for k in range(2):
            z_copy(i, k, 0)

    def z_forward(i, step):
        for k in range(2):
            z_wait(i, k, step - 1)
            z_copy(i, k, step)

    def z_end(i):
        for k in range(2):
            z_wait(i, k, last)

    def masked():
        for copy in a_copies:
            copy.wait()
        rows = amat[0].shape[0] // W
        for g in range(groups):
            def body(e, carry):
                b, p = e // rows, e % rows
                keep = mask[z * rows + p, b * groups + g].astype(F32)
                at = (pl.ds(pl.multiple_of(p * W, W), W), pl.ds(pl.multiple_of(b * W, W), W))
                amat[g][at] = (amat[g][at].astype(F32) * keep).astype(BF16)
                return carry

            lax.fori_loop(0, nz * rows, body, 0)

    step_n = 256

    def product(g):
        def body(e, carry):
            at = pl.ds(pl.multiple_of(e * step_n, step_n), step_n)
            right = uz[g][:, :, at].reshape(nz * W, step_n)
            new = jnp.dot(amat[g][...], right, preferred_element_type=F32)
            if g > 0:
                new = new + total[:, at]
            total[:, at] = new
            return carry

        lax.fori_loop(0, total.shape[1] // step_n, body, 0)

    def done_group(i):
        g, off, rows = CHUNKS[i]
        return g if off + rows == W else None

    def ring_end(i):
        z_end(i)
        if done_group(i) is not None:
            product(done_group(i))

    def ring_end(i):
        z_end(i)
        if done_group(i) is not None:
            product(done_group(i))

    to_sibling(0)
    start_own(0)
    start_sib(0)
    loaded(1)
    for i in range(1, n):
        to_sibling(i)
    for i in range(1, min(n, 2)):
        start_raw(i)
    for k in range(-4, n + 2):
        if 0 <= k + 1 < n:
            owners(k + 1)
        if 0 <= k + 2 < n:
            scatter_b(k + 2)
        if 0 <= k < n:
            z_forward(k, 1)
        if 0 <= k - 1 < n:
            z_forward(k - 1, 3)
        if 0 <= k + 3 < n:
            scatter_a(k + 3)
        if k + 6 < n:
            start_raw(k + 6)
        if k + 4 < n:
            finish_raw(k + 4)
            scatter_pair(k + 4)
        if k == -3:
            load_coupling()
        if k == min(0, n - 2):
            masked()
        if 0 <= k - 2 < n:
            ring_end(k - 2)
        if 0 <= k + 1 < n:
            z_begin(k + 1)
        if 0 <= k < n:
            z_forward(k, 2)

    for copy in sent:
        copy.wait_send()


def densities(total, dr, dc, out_r, out_c):
    blocks = dr.shape[0] // W
    for k, (dens, out) in enumerate(((dr, out_r), (dc, out_c))):
        for b in range(blocks):
            at = (k * blocks + b) * W
            s = total[:, at:at + W]
            high = s.astype(BF16)
            low = (s - high.astype(F32)).astype(BF16)
            d = dens[b * W:(b + 1) * W, :]
            out[:, b * W:(b + 1) * W] = jnp.dot(high, d, preferred_element_type=F32) + jnp.dot(
                low, d, preferred_element_type=F32)


def shards(transformed, coupling, block_mask, density_row, density_col,
           row_owner, row_slot, col_owner, col_slot):
    nz = lax.axis_size("aux")
    aux_dev, pairs = transformed.shape
    tiles = pairs // W
    slots = density_row.shape[0] // W
    columns = 2 * density_row.shape[0]
    groups = aux_dev // W
    keys = jnp.stack([(row_owner * slots + row_slot)[:, 0], (col_owner * slots + col_slot)[:, 0]])
    keys = jnp.pad(keys, ((0, 0), (0, -keys.shape[1] % W)), constant_values=-1)
    n = len(CHUNKS)
    halves = [c[2] // 2 for c in CHUNKS]
    scratch = []
    scratch += [pltpu.VMEM((2 * CORES, tiles + 1, h, W), BF16) for h in halves]
    scratch += [pltpu.VMEM((RING, 16, h, W), BF16) for h in halves]
    scratch += [pltpu.VMEM((RING, 16, h, W), BF16) for h in halves]
    scratch += [pltpu.VMEM((16, h, W), BF16) for h in halves]
    scratch += [pltpu.VMEM((2, 8, h, W), BF16) for h in halves]
    scratch += [pltpu.VMEM((2, 16, h, W), BF16) for h in halves]
    scratch += [pltpu.VMEM((2, 16, h, W), BF16) for h in halves]
    scratch += [pltpu.VMEM((h, columns), BF16) for h in halves]
    scratch += [pltpu.VMEM((nz, W, columns), BF16) for _ in range(groups)]
    scratch += [pltpu.VMEM((aux_dev, nz * W), BF16) for _ in range(groups)]
    scratch += [pltpu.VMEM((tiles, aux_dev, W), BF16)]
    scratch += [pltpu.VMEM((16, max(halves), W), F32),
                pltpu.VMEM((8 * RING * slots, W), jnp.int32),
                pltpu.SMEM((8 * RING * slots, W), jnp.int32)]
    dma = pltpu.SemaphoreType.DMA
    steps = nz // 2
    scratch += [dma((groups,)), dma((2,)), dma((n,)), dma((n, 2)), dma((n,)), dma((n, 4)), dma((n, 2)), dma((n, 2)),
                dma((n, 2)), dma((n, 2)), dma((n, 2)), dma((n, 2)), dma((n,)), dma((n,)),
                dma((n, 2, steps)), dma((n, 2, steps)), dma((1,))]
    vmem, smem = pl.BlockSpec(memory_space=pltpu.VMEM), pl.BlockSpec(memory_space=pltpu.SMEM)
    hbm = pl.BlockSpec(memory_space=pl.ANY)
    sums = pl.pallas_call(
        functools.partial(kernel, nz, tiles, slots),
        out_shape=jax.ShapeDtypeStruct((aux_dev, columns), F32),
        in_specs=[vmem, smem, hbm, hbm],
        out_specs=vmem,
        scratch_shapes=scratch,
        compiler_params=pltpu.CompilerParams(
            collective_id=0, has_side_effects=True, vmem_limit_bytes=56 * 1024 * 1024),
        cost_estimate=pl.CostEstimate(
            flops=2 * aux_dev * nz * aux_dev * columns, bytes_accessed=16 << 20,
            transcendentals=0),
    )(keys, block_mask, transformed, coupling)
    shape = jax.ShapeDtypeStruct((aux_dev, columns // 2), F32)
    whole = pl.BlockSpec(density_row.shape, lambda i: (0, 0))
    out = pl.BlockSpec((W, columns // 2), lambda i: (i, 0))
    return pl.pallas_call(
        densities, out_shape=(shape, shape), grid=(groups,),
        in_specs=[pl.BlockSpec((W, columns), lambda i: (i, 0)), whole, whole],
        out_specs=(out, out),
    )(sums, density_row, density_col)


def solution(mesh):
    placed = (P("aux", "tile"), P("aux", None), P(), P("tile", None), P("tile", None),
              P(), P(), P(), P())
    return jax.shard_map(shards, mesh=mesh, in_specs=placed,
                         out_specs=(P("aux", "tile"), P("aux", "tile")), check_vma=False)
```

```python
import functools

import jax
import jax.numpy as jnp
from jax import lax
from jax.experimental import pallas as pl
from jax.experimental.pallas import tpu as pltpu
from jax.sharding import PartitionSpec as P

RING = 4
CORES = 2
W = 128
CHUNKS = tuple((g, off, 64) for g in range(4) for off in (0, 64))
F32, BF16 = jnp.float32, jnp.bfloat16


def kernel(nz, tiles, slots, keys, mask, t_hbm, c_hbm, total, *scratch):
    n = len(CHUNKS)
    groups = c_hbm.shape[1] // (nz * W)
    it = iter(scratch)
    take = lambda k: [next(it) for _ in range(k)]
    raw, sa, ra, sb, rb, us = (take(n) for _ in range(6))
    uz = take(groups)
    amat = take(groups)
    tv, own, tbl_v, tbl = take(4)
    (a_sem, tv_sem, loc_sem, e1_send, sib_send, e1_recv, fw_send, ea_send, ea_recv, eb_send, eb_recv,
     es_send, es_recv, z_send, z_recv, tbl_sem) = take(16)

    z, t = lax.axis_index("aux"), lax.axis_index("tile")
    c, x, y = t % CORES, (t // CORES) % RING, t // (CORES * RING)

    def tid(yy, xx, cc):
        return (yy * RING + xx) * CORES + cc

    def pick(for0, for1):
        return for0 + c * (for1 - for0)

    def first(d):
        return pick(tid(y, (x + RING + d) % RING, 0), tid((y + RING + d) % RING, x, 1))

    def second(d):
        return pick(tid((y + RING + d) % RING, x, 0), tid(y, (x + RING + d) % RING, 1))

    sibling = tid(y, x, 1 - c)
    m1, m2 = pick(x, y), pick(y, x)
    g_opp, g_p, g_m = (m2 + 2) % RING, (m2 + 1) % RING, (m2 + 3) % RING
    z_to = ((z + 1) % nz, (z + nz - 1) % nz)
    sent = []

    def remote(src, dst, send, recv, zz, tt):
        return pltpu.make_async_remote_copy(
            src_ref=src, dst_ref=dst, send_sem=send, recv_sem=recv,
            device_id=(zz, tt), device_id_type=pl.DeviceIdType.MESH)

    def go(src, dst, send, recv, zz, tt):
        copy = remote(src, dst, send, recv, zz, tt)
        copy.start()
        sent.append(copy)

    def arrived(ref, recv):
        remote(ref, ref, a_sem.at[0], recv, z, sibling).wait_recv()

    def rows_of(i, h):
        g, off, rows = CHUNKS[i]
        return pl.ds(pl.multiple_of(g * W + off + h * (rows // 2), 16), rows // 2)

    def slot(i, s):
        return raw[i].at[s, pl.ds(0, tiles)]

    head = CHUNKS[0][2]
    spans = (pl.ds(0, head), pl.ds(head, tv.shape[1] - head))

    def load_tiles(k):
        def body(e, carry):
            pltpu.make_async_copy(
                t_hbm.at[spans[k], pl.ds(pl.multiple_of(e * W, W), W)],
                tv.at[e, spans[k]], tv_sem.at[k]).start()
            return carry

        lax.fori_loop(0, tiles, body, 0)

    def loaded(k):
        span = tv.at[:, spans[k]]
        pltpu.make_async_copy(span, span, tv_sem.at[k]).wait()

    a_copies = []

    def load_coupling():
        for g in range(groups):
            for b in range(nz):
                copy = pltpu.make_async_copy(
                    c_hbm.at[:, pl.ds((b * groups + g) * W, W)],
                    amat[g].at[:, pl.ds(b * W, W)], a_sem.at[g])
                copy.start()
                a_copies.append(copy)

    def empty_tiles(i):
        for s in range(2 * RING):
            raw[i][s, tiles] = jnp.zeros(raw[i].shape[2:], BF16)

    def build_table():
        half = 2 * RING * slots
        row = lax.broadcasted_iota(jnp.int32, (half, 1), 0)
        gg, co, sl = row // (CORES * slots), row // slots % CORES, row % slots
        want = pick((gg * RING + x) * CORES + co, (y * RING + gg) * CORES + co) * slots + sl
        lane = lax.broadcasted_iota(jnp.int32, (half, keys.shape[1]), 1)
        entry = lax.broadcasted_iota(jnp.int32, (half, W), 1)
        for side in range(2):
            hit = keys[side:side + 1, :] == want
            table = jnp.zeros((half, W), jnp.int32)
            for s in range(2 * RING):
                a = (m1 + s // CORES) % RING
                low = tid(pick(y, a), pick(a, x), s % CORES) * tiles
                here = hit & (lane >= low) & (lane < low + tiles)
                least = jnp.min(jnp.where(here, lane, 1 << 20), axis=1, keepdims=True)
                most = jnp.max(jnp.where(here, lane, -1), axis=1, keepdims=True)
                k0 = jnp.where(most >= 0, least - low, tiles)
                k1 = jnp.where(most > least, most - low, tiles)
                table = jnp.where(entry == 2 * s, k0, jnp.where(entry == 2 * s + 1, k1, table))
            tbl_v[side * half:(side + 1) * half, :] = table
        copy = pltpu.make_async_copy(tbl_v, tbl, tbl_sem.at[0])
        copy.start()
        copy.wait()

    barrier = pltpu.get_barrier_semaphore()
    near = [(z, sibling), (z_to[0], t), (z_to[1], t)]
    for d in (1, -1):
        near.append((z, first(d)))
        near.append((z, second(d)))
    for who in near:
        pl.semaphore_signal(barrier, inc=1, device_id=who, device_id_type=pl.DeviceIdType.MESH)
    load_tiles(0)
    empty_tiles(0)
    pl.semaphore_wait(barrier, len(near))

    def local(i):
        return pltpu.make_async_copy(tv.at[:, rows_of(i, c)], slot(i, c), loc_sem.at[i])

    def to_sibling(i):
        go(tv.at[:, rows_of(i, 1 - c)], slot(i, c), sib_send.at[i], e1_recv.at[i, c], z, sibling)
        local(i).start()

    def start_own(i):
        send_raw(i, 0, c, tv.at[:, rows_of(i, c)])

    def start_sib(i):
        arrived(slot(i, 1 - c), e1_recv.at[i, 1 - c])
        send_raw(i, 1, 1 - c, slot(i, 1 - c))

    def send_raw(i, k, cc, src):
        for m, d in enumerate((1, -1)):
            s = ((RING - d) % RING) * CORES + cc
            go(src, slot(i, s), e1_send.at[i, 2 * k + m], e1_recv.at[i, s], z, first(d))

    def start_raw(i):
        start_own(i)
        start_sib(i)

    def forward_raw(i):
        for m, (d, s, cc) in enumerate(((1, 6 + c, c), (-1, 2 + 1 - c, 1 - c))):
            arrived(slot(i, s), e1_recv.at[i, s])
            go(slot(i, s), slot(i, 4 + cc), fw_send.at[i, m], e1_recv.at[i, 4 + cc], z, first(d))

    def finish_raw(i):
        local(i).wait()
        for s in (6 + 1 - c, 2 + c, 4, 5):
            arrived(slot(i, s), e1_recv.at[i, s])

    def summed(i, g, j):
        acc = None
        row = (j // slots % 2) * (2 * RING * slots) + (g * CORES + j // (2 * slots)) * slots + j % slots
        for e in range(4 * RING):
            v = raw[i][e // 2, tbl[row, e]].astype(F32)
            acc = v if acc is None else acc + v
        return acc

    def fill(i, g, low, high, store, extra=None):
        def body(j, carry):
            v = summed(i, g, j)
            if extra is not None:
                v = v + extra[j - low].astype(F32)
            store[j] = v.astype(store.dtype)
            return carry

        lax.fori_loop(low, high, body, 0)

    def scatter_a(i):
        fill(i, g_opp, 0, 16, sa[i])
        go(sa[i].at[pl.ds(0, 8)], ra[i].at[0], ea_send.at[i, 0], ea_recv.at[i, 0], z, second(1))
        go(sa[i].at[pl.ds(8, 8)], ra[i].at[1], ea_send.at[i, 1], ea_recv.at[i, 1], z, second(-1))

    def scatter_b(i):
        fill(i, g_p, 8, 16, sb[i].at[0])
        fill(i, g_m, 0, 8, sb[i].at[1])
        arrived(ra[i].at[0], ea_recv.at[i, 0])
        fill(i, g_p, 0, 8, sb[i].at[0], ra[i].at[0])
        go(sb[i].at[0], rb[i].at[0], eb_send.at[i, 0], eb_recv.at[i, 0], z, second(1))
        arrived(ra[i].at[1], ea_recv.at[i, 1])
        fill(i, g_m, 8, 16, sb[i].at[1], ra[i].at[1])
        go(sb[i].at[1], rb[i].at[1], eb_send.at[i, 1], eb_recv.at[i, 1], z, second(-1))
        fill(i, m2, 0, 16, own.at[:, pl.ds(0, CHUNKS[i][2] // 2)])

    def part(i, zz, first_row, rows):
        g, off, _ = CHUNKS[i]
        return uz[g].at[zz, pl.ds(pl.multiple_of(off + first_row, 16), rows)]

    def owners(i):
        g, off, rows = CHUNKS[i]
        half = rows // 2
        mine = pl.ds(pl.multiple_of(off + c * half, 16), half)
        for k in range(2):
            arrived(rb[i].at[k], eb_recv.at[i, k])

        def position(j):
            return own[j, :half] + rb[i][0, j].astype(F32) + rb[i][1, j].astype(F32)

        for jj in range(8):
            us[i][:, jj * W:(jj + 1) * W] = position((1 - c) * 8 + jj).astype(BF16)
        go(us[i], part(i, z, c * half, half), es_send.at[i], es_recv.at[i], z, sibling)
        for jj in range(8):
            uz[g][z, mine, jj * W:(jj + 1) * W] = position(c * 8 + jj).astype(BF16)

    last = nz // 2 - 1

    def z_part(i, k, step, origin):
        rows = CHUNKS[i][2]
        if step == last:
            return part(i, origin, k * (rows // 2), rows // 2)
        return part(i, origin, 0, rows)

    def z_copy(i, k, step):
        ref = z_part(i, k, step, (z + (nz - step if k == 0 else step)) % nz)
        go(ref, ref, z_send.at[i, k, step], z_recv.at[i, k, step], z_to[k], t)

    def z_wait(i, k, step):
        origin = (z + (2 * nz - 1 - step if k == 0 else step + 1)) % nz
        arrived(z_part(i, k, step, origin), z_recv.at[i, k, step])

    def z_begin(i):
        half = CHUNKS[i][2] // 2
        arrived(part(i, z, (1 - c) * half, half), es_recv.at[i])
        for k in range(2):
            z_copy(i, k, 0)

    def z_forward(i, step):
        for k in range(2):
            z_wait(i, k, step - 1)
            z_copy(i, k, step)

    def z_end(i):
        for k in range(2):
            z_wait(i, k, last)

    def masked():
        for copy in a_copies:
            copy.wait()
        rows = amat[0].shape[0] // W
        for g in range(groups):
            def body(e, carry):
                b, p = e // rows, e % rows
                keep = mask[z * rows + p, b * groups + g].astype(F32)
                at = (pl.ds(pl.multiple_of(p * W, W), W), pl.ds(pl.multiple_of(b * W, W), W))
                amat[g][at] = (amat[g][at].astype(F32) * keep).astype(BF16)
                return carry

            lax.fori_loop(0, nz * rows, body, 0)

    step_n = 256

    def product(g):
        def body(e, carry):
            at = pl.ds(pl.multiple_of(e * step_n, step_n), step_n)
            right = uz[g][:, :, at].reshape(nz * W, step_n)
            new = jnp.dot(amat[g][...], right, preferred_element_type=F32)
            if g > 0:
                new = new + total[:, at]
            total[:, at] = new
            return carry

        lax.fori_loop(0, total.shape[1] // step_n, body, 0)

    def done_group(i):
        g, off, rows = CHUNKS[i]
        return g if off + rows == W else None

    def ring_end(i):
        z_end(i)
        if done_group(i) is not None:
            product(done_group(i))

    def ring_end(i):
        z_end(i)
        if done_group(i) is not None:
            product(done_group(i))

    loaded(0)
    to_sibling(0)
    start_own(0)
    load_tiles(1)
    start_sib(0)
    load_coupling()
    build_table()
    loaded(1)
    for i in range(1, n):
        to_sibling(i)
    forward_raw(0)
    for i in range(1, min(n, 3)):
        start_raw(i)
    for i in range(1, n):
        empty_tiles(i)
    for k in range(-2, n + 2):
        if k > -2:
            if k + 3 < n:
                forward_raw(k + 3)
            if k + 5 < n:
                start_raw(k + 5)
        if k + 2 < n:
            finish_raw(k + 2)
            scatter_a(k + 2)
        if k == -2:
            if n > 1:
                forward_raw(1)
            if n > 3:
                start_raw(3)
        if 0 <= k + 1 < n:
            owners(k + 1)
        if 0 <= k - 2 < n:
            ring_end(k - 2)
        if 0 <= k + 1 < n:
            z_begin(k + 1)
        if 0 <= k < n:
            z_forward(k, 2)
        if k + 2 < n:
            scatter_b(k + 2)
        if k == -1:
            masked()
        if 0 <= k + 1 < n:
            z_forward(k + 1, 1)
        if 0 <= k < n:
            z_forward(k, 3)

    for copy in sent:
        copy.wait_send()


def densities(total, dr, dc, out_r, out_c):
    blocks = dr.shape[0] // W
    for k, (dens, out) in enumerate(((dr, out_r), (dc, out_c))):
        for b in range(blocks):
            at = (k * blocks + b) * W
            s = total[:, at:at + W]
            high = s.astype(BF16)
            low = (s - high.astype(F32)).astype(BF16)
            d = dens[b * W:(b + 1) * W, :]
            out[:, b * W:(b + 1) * W] = jnp.dot(high, d, preferred_element_type=F32) + jnp.dot(
                low, d, preferred_element_type=F32)


def shards(transformed, coupling, block_mask, density_row, density_col,
           row_owner, row_slot, col_owner, col_slot):
    nz = lax.axis_size("aux")
    aux_dev, pairs = transformed.shape
    tiles = pairs // W
    slots = density_row.shape[0] // W
    columns = 2 * density_row.shape[0]
    groups = aux_dev // W
    keys = jnp.stack([(row_owner * slots + row_slot)[:, 0], (col_owner * slots + col_slot)[:, 0]])
    keys = jnp.pad(keys, ((0, 0), (0, -keys.shape[1] % W)), constant_values=-1)
    n = len(CHUNKS)
    halves = [c[2] // 2 for c in CHUNKS]
    scratch = []
    scratch += [pltpu.VMEM((2 * RING, tiles + 1, h, W), BF16) for h in halves]
    scratch += [pltpu.VMEM((16, h, W), BF16) for h in halves]
    scratch += [pltpu.VMEM((2, 8, h, W), BF16) for h in halves]
    scratch += [pltpu.VMEM((2, 16, h, W), BF16) for h in halves]
    scratch += [pltpu.VMEM((2, 16, h, W), BF16) for h in halves]
    scratch += [pltpu.VMEM((h, columns), BF16) for h in halves]
    scratch += [pltpu.VMEM((nz, W, columns), BF16) for _ in range(groups)]
    scratch += [pltpu.VMEM((aux_dev, nz * W), BF16) for _ in range(groups)]
    scratch += [pltpu.VMEM((tiles, aux_dev, W), BF16)]
    scratch += [pltpu.VMEM((16, max(halves), W), F32),
                pltpu.VMEM((4 * RING * slots, W), jnp.int32),
                pltpu.SMEM((4 * RING * slots, W), jnp.int32)]
    dma = pltpu.SemaphoreType.DMA
    steps = nz // 2
    scratch += [dma((groups,)), dma((2,)), dma((n,)), dma((n, 4)), dma((n,)), dma((n, 8)), dma((n, 2)),
                dma((n, 2)), dma((n, 2)), dma((n, 2)), dma((n, 2)), dma((n,)), dma((n,)),
                dma((n, 2, steps)), dma((n, 2, steps)), dma((1,))]
    vmem, smem = pl.BlockSpec(memory_space=pltpu.VMEM), pl.BlockSpec(memory_space=pltpu.SMEM)
    hbm = pl.BlockSpec(memory_space=pl.ANY)
    sums = pl.pallas_call(
        functools.partial(kernel, nz, tiles, slots),
        out_shape=jax.ShapeDtypeStruct((aux_dev, columns), F32),
        in_specs=[vmem, smem, hbm, hbm],
        out_specs=vmem,
        scratch_shapes=scratch,
        compiler_params=pltpu.CompilerParams(
            collective_id=0, has_side_effects=True, vmem_limit_bytes=56 * 1024 * 1024),
        cost_estimate=pl.CostEstimate(
            flops=2 * aux_dev * nz * aux_dev * columns, bytes_accessed=16 << 20,
            transcendentals=0),
    )(keys, block_mask, transformed, coupling)
    shape = jax.ShapeDtypeStruct((aux_dev, columns // 2), F32)
    whole = pl.BlockSpec(density_row.shape, lambda i: (0, 0))
    out = pl.BlockSpec((W, columns // 2), lambda i: (i, 0))
    return pl.pallas_call(
        densities, out_shape=(shape, shape), grid=(groups,),
        in_specs=[pl.BlockSpec((W, columns), lambda i: (i, 0)), whole, whole],
        out_specs=(out, out),
    )(sums, density_row, density_col)


def solution(mesh):
    placed = (P("aux", "tile"), P("aux", None), P(), P("tile", None), P("tile", None),
              P(), P(), P(), P())
    return jax.shard_map(shards, mesh=mesh, in_specs=placed,
                         out_specs=(P("aux", "tile"), P("aux", "tile")), check_vma=False)
```
